32 devices in a mesh: grp: 4 (over z), dev: 8 (over y, x, core).
Axes of the slice: x: 2, y: 2, z: 4, core: 2. Of those that a mesh axis runs over, the one named last changes fastest.
Arguments:
- points: float32 [3, 524288], P(None, ('grp', 'dev')), may hold values from -6 to 6
- rhs: float32 [32, 524288], P(None, ('grp', 'dev')), may hold values from -6 to 6
- leaf_count: int32 [2048], P(('grp', 'dev')), may hold values from 64 to 256
- near_list: int32 [2048, 8], P(('grp', 'dev')), may hold values from 0 to 2047, as said below
- leaf_basis: float32 [64, 524288], P(None, ('grp', 'dev')), may hold values from -0.375 to 0.375
- leaf_transfer: float32 [64, 131072], P(None, ('grp', 'dev')), may hold values from -0.75 to 0.75
- leaf_parent: int32 [2048], P(('grp', 'dev')), may hold values from 0 to 255, as said below
- nodes1: float32 [3, 16384], P(None, ('grp', 'dev')), may hold values from -6 to 6
- box_transfer: float32 [64, 16384], P(None, ('grp', 'dev')), may hold values from -0.75 to 0.75
- box_parent: int32 [256], P(('grp', 'dev')), may hold values from 0 to 31, as said below
- far1: int32 [256, 16], P(('grp', 'dev')), may hold values from 0 to 255, as said below
- nodes2: float32 [3, 2048], replicated, may hold values from -6 to 6
- far2: int32 [32, 8], replicated, may hold values from 0 to 31, as said below
Outputs:
- result: float32 [32, 524288], P(None, ('grp', 'dev'))
The draws below stay inside these ranges and needn't reach their ends.
Inputs may be any that keep to these rules, and one draw needn't show every extreme that they name: `near_list`: row c begins with c itself; its other 7 entries are distinct leaf blocks of the same group of 512 blocks (c // 512 alike), each different from c by at most 32. `leaf_parent`: leaf c's box lies on the same device: it is one of boxes (c // 64) * 8 to (c // 64 + 1) * 8 - 1, and every box has exactly 8 leaves. `box_parent`: box b's parent belongs to its group: it is one of (b // 64) * 8 to (b // 64 + 1) * 8 - 1, and every level-2 box has exactly 8 children. `far1`: row t names 16 distinct level-1 boxes of t's group (b // 64 alike), never t. `far2`: row t names 8 distinct level-2 boxes, never t.
All inputs are finite; a program needn't handle non-finite values.
Results may differ from the reference program's by a relative error of at most 0.00011.
Values sent between devices are 32-bit elements; how exact they have to be, the bound alone decides.
No kernel may reach another device: no remote copies, remote signals or barrier semaphores. Data moves between devices by JAX's collectives and lax.ppermute only.
A program may use at most 128 MiB of HBM per device.

```python
import jax
import jax.numpy as jnp
from jax import lax

B = 256
K = 64
R = 32
LEAF_DEV = 64
NEAR = 8
CHILD = 8
FAR1 = 16
FAR2 = 8
REACH = 32
BOX1_DEV = 8
B2_GRP = 8
GLEAVES = 512
G1 = 64
LEAVES = 2048
NPTS = 524288
NB1 = 256
NB2 = 32


def draw_near_list(key, part):
    key = jax.random.fold_in(key, 101)
    leaf = jnp.arange(LEAVES, dtype=jnp.int32)
    start = leaf // GLEAVES * GLEAVES
    offsets = jnp.concatenate([jnp.arange(-REACH, 0, dtype=jnp.int32), jnp.arange(1, REACH + 1, dtype=jnp.int32)])
    keys = jax.random.split(key, LEAVES)

    def single(sub, own, first):
        order = jax.random.permutation(sub, offsets)
        target = own + order
        outside = ((target < first) | (target >= first + GLEAVES)).astype(jnp.int32)
        pick = jnp.argsort(outside, stable=True)[:NEAR - 1]
        return jnp.concatenate([own[None], target[pick]]).astype(jnp.int32)
    return jax.vmap(single)(keys, leaf, start)


def draw_leaf_parent(key, part):
    key = jax.random.fold_in(key, 202)
    count = LEAVES // LEAF_DEV
    keys = jax.random.split(key, count)

    def single(sub, device):
        order = jax.random.permutation(sub, LEAF_DEV).astype(jnp.int32)
        return device * BOX1_DEV + order // CHILD
    return jax.vmap(single)(keys, jnp.arange(count, dtype=jnp.int32)).reshape(LEAVES).astype(jnp.int32)


def draw_box_parent(key, part):
    key = jax.random.fold_in(key, 303)
    count = NB1 // G1
    keys = jax.random.split(key, count)

    def single(sub, group):
        order = jax.random.permutation(sub, G1).astype(jnp.int32)
        return group * B2_GRP + order // CHILD
    return jax.vmap(single)(keys, jnp.arange(count, dtype=jnp.int32)).reshape(NB1).astype(jnp.int32)


def draw_far1(key, part):
    key = jax.random.fold_in(key, 404)
    boxes = jnp.arange(NB1, dtype=jnp.int32)
    keys = jax.random.split(key, NB1)
    steps_all = jnp.arange(1, G1, dtype=jnp.int32)

    def single(sub, box):
        order = jax.random.permutation(sub, steps_all)[:FAR1]
        first = box // G1 * G1
        return (first + (box - first + order) % G1).astype(jnp.int32)
    return jax.vmap(single)(keys, boxes)


def draw_far2(key, part):
    key = jax.random.fold_in(key, 505)
    boxes = jnp.arange(NB2, dtype=jnp.int32)
    keys = jax.random.split(key, NB2)
    steps_all = jnp.arange(1, NB2, dtype=jnp.int32)

    def single(sub, box):
        order = jax.random.permutation(sub, steps_all)[:FAR2]
        return ((box + order) % NB2).astype(jnp.int32)
    return jax.vmap(single)(keys, boxes)


def set_ends(values, own_key, smallest, largest):
    longest = values.shape.index(max(values.shape))
    spots = []
    for shift in (0, 1):
        where = [jax.random.randint(jax.random.fold_in(own_key, axis), (), 0, length) for axis, length in enumerate(values.shape)]
        where[longest] = (where[longest] + shift) % values.shape[longest]
        spots.append(tuple(where))
    return values.at[spots[0]].set(smallest).at[spots[1]].set(largest)


def steps_of(stream_key, dims, cuts, smallest, largest):
    def one(position, parts):
        steps = jax.random.uniform(jax.random.fold_in(jax.random.fold_in(stream_key, 6), position), (parts,), jnp.float32, smallest / len(cuts), largest / len(cuts))
        return jnp.repeat(jnp.exp(steps), dims[position] // parts).reshape((-1,) + (1,) * (len(dims) - position - 1))

    gain = one(*cuts[0])
    for cut in cuts[1:]:
        gain = gain * one(*cut)
    return gain


def noise(stream_key, dims, width, bound, cuts=(), held_as=jnp.bfloat16):
    gain = steps_of(stream_key, dims, cuts, -0.22, 0.18) if cuts else 1.0
    entries = jax.random.normal(stream_key, dims, jnp.float32) * width * gain
    return jnp.minimum(jnp.maximum(entries, -bound), bound).astype(held_as)


def setup_inputs(seed: int = 0) -> dict:
    arg_keys = jax.random.split(jax.random.key(seed), 14)
    points = noise(arg_keys[0], (3, NPTS), 1.0, 6.0, ((1, 32),), jnp.float32)
    rhs = noise(arg_keys[1], (R, NPTS), 1.0, 6.0, ((1, 32),), jnp.float32)
    leaf_count = set_ends(jax.random.randint(arg_keys[2], (LEAVES,), B // 4, B + 1), jax.random.fold_in(arg_keys[2], 1), B // 4, B).astype(jnp.int32)
    near_list = draw_near_list(jax.random.fold_in(arg_keys[13], 71), 0)
    leaf_basis = noise(arg_keys[4], (K, NPTS), B ** -0.5, 0.375, ((1, 32),), jnp.float32)
    leaf_transfer = noise(arg_keys[5], (K, LEAVES * K), K ** -0.5, 0.75, ((1, 32),), jnp.float32)
    leaf_parent = draw_leaf_parent(jax.random.fold_in(arg_keys[13], 71), 0)
    nodes1 = noise(arg_keys[7], (3, NB1 * K), 1.0, 6.0, ((1, 32),), jnp.float32)
    box_transfer = noise(arg_keys[8], (K, NB1 * K), K ** -0.5, 0.75, ((1, 32),), jnp.float32)
    box_parent = draw_box_parent(jax.random.fold_in(arg_keys[13], 71), 0)
    far1 = draw_far1(jax.random.fold_in(arg_keys[13], 71), 0)
    nodes2 = noise(arg_keys[11], (3, NB2 * K), 1.0, 6.0, (), jnp.float32)
    far2 = draw_far2(jax.random.fold_in(arg_keys[13], 71), 0)
    return {"points": points, "rhs": rhs, "leaf_count": leaf_count, "near_list": near_list, "leaf_basis": leaf_basis, "leaf_transfer": leaf_transfer, "leaf_parent": leaf_parent, "nodes1": nodes1, "box_transfer": box_transfer, "box_parent": box_parent, "far1": far1, "nodes2": nodes2, "far2": far2}


HIGH = lax.Precision.HIGHEST

def kernel(first, second):
    d_zero = first[0][:, None] - second[0][None, :]
    d_one = first[1][:, None] - second[1][None, :]
    d_two = first[2][:, None] - second[2][None, :]
    dist = d_zero * d_zero + d_one * d_one + d_two * d_two
    return lax.rsqrt(1.0 + 16.0 * dist)

def reference(points, rhs, leaf_count, near_list, leaf_basis, leaf_transfer, leaf_parent, nodes1, box_transfer, box_parent, far1, nodes2, far2):
    slots = jnp.arange(B, dtype=jnp.int32)
    mask = (slots[None, :] < leaf_count[:, None]).astype(jnp.float32)
    leaf_points = points.reshape(3, LEAVES, B).transpose(1, 0, 2)
    values = rhs.reshape(R, LEAVES, B).transpose(1, 0, 2) * mask[:, None, :]

    def near_leaf(own, index):
        source_points = leaf_points[index]
        source_values = values[index]
        tiles = jax.vmap(lambda src: kernel(src, own))(source_points)
        return jnp.einsum('nrj,nji->ri', source_values, tiles, precision=HIGH)

    def near_block(inputs):
        return jax.vmap(near_leaf)(inputs[0], inputs[1])
    blocks = LEAVES // LEAF_DEV
    near = lax.map(near_block, (leaf_points.reshape(blocks, LEAF_DEV, 3, B), near_list.reshape(blocks, LEAF_DEV, NEAR)))
    near = near.reshape(LEAVES, R, B)
    basis = leaf_basis.reshape(K, LEAVES, B).transpose(1, 0, 2)
    m_leaf = jnp.einsum('lkb,lrb->lkr', basis, values, precision=HIGH)
    e_mats = leaf_transfer.reshape(K, LEAVES, K).transpose(1, 0, 2)
    lifted = jnp.einsum('lij,lir->ljr', e_mats, m_leaf, precision=HIGH)
    m_one = jax.ops.segment_sum(lifted, leaf_parent, NB1)
    f_mats = box_transfer.reshape(K, NB1, K).transpose(1, 0, 2)
    raised = jnp.einsum('bij,bir->bjr', f_mats, m_one, precision=HIGH)
    m_two = jax.ops.segment_sum(raised, box_parent, NB2)
    node_one = nodes1.reshape(3, NB1, K).transpose(1, 0, 2)
    node_two = nodes2.reshape(3, NB2, K).transpose(1, 0, 2)

    def couple(target, sources, expansions):
        tiles = jax.vmap(lambda src: kernel(target, src))(sources)
        return jnp.einsum('sij,sjr->ir', tiles, expansions, precision=HIGH)
    l_one = jax.vmap(lambda t, idx: couple(t, node_one[idx], m_one[idx]))(node_one, far1)
    l_two = jax.vmap(lambda t, idx: couple(t, node_two[idx], m_two[idx]))(node_two, far2)
    g_one = l_one + jnp.einsum('bij,bjr->bir', f_mats, l_two[box_parent], precision=HIGH)
    g_leaf = jnp.einsum('lij,ljr->lir', e_mats, g_one[leaf_parent], precision=HIGH)
    far_part = jnp.einsum('lkr,lkb->lrb', g_leaf, basis, precision=HIGH)
    total = (near + far_part) * mask[:, None, :]
    return total.transpose(1, 0, 2).reshape(R, NPTS)
```

```python
import jax
import jax.numpy as jnp
from jax import lax
from jax.experimental import pallas as pl
from jax.experimental.pallas import tpu as pltpu
from jax.sharding import PartitionSpec as P

B = 256
K = 64
R = 32
NEAR = 8
CHILD = 8
REACH = 32
ROWS = 16
PER = B // ROWS
UNROLL = 8
SPAN = NEAR * PER + PER

F32 = jnp.float32
BF16 = jnp.bfloat16
HIGH = lax.Precision.HIGHEST
LIMIT = 58 * 1024 * 1024

PIECES = ((0, 0), (0, 1), (1, 0), (1, 1), (0, 2), (2, 0), (1, 2), (2, 1))


def params():
    return pltpu.CompilerParams(vmem_limit_bytes=LIMIT)


def vmem():
    return pl.BlockSpec(memory_space=pltpu.VMEM)


def smem():
    return pl.BlockSpec(memory_space=pltpu.SMEM)


def split(x):
    high = x.astype(BF16)
    return high, (x - high.astype(F32)).astype(BF16)


def to_grid(x, step):
    big = 1.5 * 2.0**23 * step
    return (x + big) - big


def dot(a, b):
    return jnp.dot(a, b, preferred_element_type=F32)


def dot_nt(a, b):
    return lax.dot_general(a, b, (((1,), (1,)), ((), ())), preferred_element_type=F32)


def features(coords, targets=True):
    n = coords.shape[1]
    scaled = jnp.concatenate([coords * 4.0, jnp.zeros((5, n), F32)], axis=0)
    one = to_grid(scaled, 2.0**-3)
    rest = scaled - one
    two = to_grid(rest, 2.0**-11)
    three = rest - two
    pieces = (one, two, three)
    square = jnp.sum(one * one, axis=0, keepdims=True)
    s_one = to_grid(square, 8.0)
    s_two = square - s_one
    tail = jnp.sum(rest * (scaled + one), axis=0, keepdims=True)
    q_one = to_grid(tail, 2.0**-4)
    tail = tail - q_one
    q_two = to_grid(tail, 2.0**-12)
    norms = (s_one, s_two, q_one, q_two, tail - q_two)
    row = lax.broadcasted_iota(jnp.int32, (8, n), 0)
    sources, wanted = [], []
    for at, (first, second) in enumerate(PIECES):
        src = pieces[first]
        tgt = pieces[second] * -2.0
        if at < 5:
            src = jnp.where(row == 3, norms[at], jnp.where(row == 4, 1.0, src))
            tgt = jnp.where(row == 3, 1.0, jnp.where(row == 4, norms[at], tgt))
        elif at == 5:
            src = jnp.where(row == 3, 1.0, src)
            tgt = jnp.where(row == 3, 1.0, tgt)
        sources.append(src)
        wanted.append(tgt)
    source = jnp.concatenate(sources, axis=0).astype(BF16)
    if not targets:
        return source, None
    return source, jnp.concatenate(wanted, axis=0).astype(BF16)


def masked(x, count):
    slot = lax.broadcasted_iota(jnp.int32, x.shape, 1)
    return jnp.where(slot < count, x, 0.0)


def null_rows(table, start):
    source, _ = features(jnp.zeros((3, B), F32), False)
    rows = jnp.concatenate([source, jnp.zeros((2 * R, B), BF16)], axis=0).T
    table[start : start + ROWS, :] = rows[:ROWS, :]


def upward(boxes, coarse, group_of, points, rhs, basis, transfer, nodes, lower, counts, parents, uppers, offset, table, wanted, sent, left, right, top):
    del group_of
    leaves = points.shape[1] // B
    left[...] = jnp.zeros_like(left)
    right[...] = jnp.zeros_like(right)
    top[...] = jnp.zeros_like(top)
    null_rows(table, leaves * B)

    def pair(at):
        rows = []
        for side in range(2):
            c = at * 2 + side
            where = pl.ds(pl.multiple_of(c * B, B), B)
            x = masked(rhs[:, where], counts[c])
            x_two = jnp.concatenate(split(x), axis=0)
            source, target = features(points[:, where])
            wanted[c] = target
            table[where, :] = jnp.concatenate([source, x_two], axis=0).T
            b_two = jnp.concatenate(split(basis[:, where]), axis=0)
            r = dot_nt(x_two, b_two)
            rows.append(r[:R, :K] + r[:R, K:] + r[R:, :K])
        m = jnp.concatenate(rows, axis=0)
        high, low = split(m)
        left_side = jnp.concatenate(
            [jnp.concatenate([high, high], axis=1), jnp.concatenate([low, low], axis=1)], axis=0
        )
        e_two = jnp.concatenate(split(transfer[:, pl.ds(pl.multiple_of(at * 2 * K, 2 * K), 2 * K)]), axis=0)
        lifted = dot(left_side, e_two)
        lifted = lifted[: 2 * R] + lifted[2 * R :]
        p_zero = parents[at * 2] - offset[0]
        p_one = parents[at * 2 + 1] - offset[0]
        left[p_zero] += lifted[:R]
        right[p_one] += lifted[R:]

    group = 4

    def step(i, carry):
        for q in range(group):
            pair(i * group + q)
        return carry

    lax.fori_loop(0, leaves // 2 // group, step, 0)
    m_one = [left[b][:, :K] + right[b][:, K:] for b in range(boxes)]
    for b in range(boxes):
        f = lower[:, (b // 2) * 2 * K : (b // 2 + 1) * 2 * K]
        raised = jnp.dot(m_one[b], f, precision=HIGH, preferred_element_type=F32)
        raised = raised[:, (b % 2) * K : (b % 2 + 1) * K]
        top[uppers[b] - offset[1]] += raised
    zero = jnp.zeros((8, sent.shape[1]), F32)
    sent[K : K + 8, :] = zero
    sent[K : K + 3, : boxes * K] = nodes[...]
    for q in range(boxes // 4):
        block = jnp.concatenate(m_one[4 * q : 4 * q + 4], axis=0)
        sent[:K, q * 4 * R : (q + 1) * 4 * R] = block.T
    for q in range(coarse // 4):
        block = jnp.concatenate([top[4 * q + z] for z in range(4)], axis=0)
        sent[:K, (boxes + 4 * q) * R : (boxes + 4 * q + 4) * R] = block.T


def near_items(items, rows_of, table, wanted, out, kept, highs, lows, total):
    def first(t, s):
        code = items[t]
        c = code // 16
        base = (code % 16) * PER
        rows = jnp.concatenate(
            [table[pl.ds(pl.multiple_of(rows_of[c, base + q], ROWS), ROWS), :] for q in range(PER)], axis=0
        )
        kept[s][...] = rows
        u = dot(rows[:, :K], wanted[c])
        high, low = split(lax.rsqrt(u))
        highs[s][...] = high
        lows[s][...] = low

    def second(t, s):
        c = items[t] // 16
        x = kept[s][...].T[K:]
        a = dot(x, highs[s][...])
        b = dot(x[:R], lows[s][...])
        out[c] += a[:R] + a[R:] + b

    groups = (total + UNROLL - 1) // UNROLL

    @pl.when(groups > 0)
    def _():
        for q in range(UNROLL):
            first(q, q)

        def step(g, carry):
            for q in range(UNROLL):
                second((g - 1) * UNROLL + q, q)
                first(g * UNROLL + q, q)
            return carry

        lax.fori_loop(1, groups, step, 0)
        for q in range(UNROLL):
            second((groups - 1) * UNROLL + q, q)


def near_own(items, rows_of, total, table, wanted, out, *scratch):
    kept, highs, lows = scratch[:UNROLL], scratch[UNROLL : 2 * UNROLL], scratch[2 * UNROLL :]
    out[...] = jnp.zeros_like(out)
    near_items(items, rows_of, table, wanted, out, kept, highs, lows, total[0])


def near_halo(items, rows_of, total, counts, before, after, wanted, begun, out, table, *scratch):
    kept, highs, lows = scratch[:UNROLL], scratch[UNROLL : 2 * UNROLL], scratch[2 * UNROLL :]
    null_rows(table, 2 * REACH * B)
    out[...] = begun[...]

    for part, data in ((0, before), (1, after)):

        def step(i, carry, part=part, data=data):
            for q in range(4):
                c = i * 4 + q
                where = pl.ds(pl.multiple_of(c * B, B), B)
                x = masked(data[:R, where], counts[part * REACH + c])
                source, _ = features(data[R : R + 3, where], False)
                to = pl.ds(pl.multiple_of((part * REACH + c) * B, B), B)
                table[to, :] = jnp.concatenate([source, *split(x)], axis=0).T
            return carry

        lax.fori_loop(0, REACH // 4, step, 0)
    near_items(items, rows_of, table, wanted, out, kept, highs, lows, total[0])


def couple(t_nodes, s_nodes, expansions):
    tiles = []
    for s in s_nodes:
        d = [t_nodes[q] - s[q : q + 1] for q in range(3)]
        tiles.append(lax.rsqrt(1.0 + (d[0] * d[0] + d[1] * d[1] + d[2] * d[2])))
    high, low = split(jnp.concatenate(tiles, axis=1))
    r = dot(jnp.concatenate([high, low], axis=0), expansions)
    return r[:K, :R] + r[:K, R:] + r[K:, :R]


def downward(
    boxes, coarse, n_dev, n_grp, far_one, far_two, counts, parents, uppers, where_am, *refs
):
    sent = refs[:n_dev]
    tops = refs[n_dev : n_dev + n_grp]
    basis, transfer, lower, own_nodes, two_rows, two_cols, near, out = refs[n_dev + n_grp : n_dev + n_grp + 8]
    m_one, m_two, n_one, l_two, g_left, g_right = refs[n_dev + n_grp + 8 :]
    dev, grp, box_base, coarse_base, group_base = [where_am[q] for q in range(5)]
    for k in range(n_dev):
        at = lax.rem(dev - k + n_dev, n_dev)
        data = sent[k]
        for b in range(boxes):
            m_one[at * boxes + b] = jnp.concatenate(split(data[:K, b * R : (b + 1) * R]), axis=1)
            n_one[at * boxes + b] = data[K : K + 8, b * K : (b + 1) * K] * 4.0
    for k in range(n_grp):
        at = lax.rem(grp - k + n_grp, n_grp)
        data = tops[k]
        for b in range(coarse):
            m_two[at * coarse + b] = jnp.concatenate(split(data[:, b * R : (b + 1) * R]), axis=1)

    def level_two(t, carry):
        a = coarse_base + t
        index = [far_two[a, q] for q in range(far_two.shape[1])]
        start = pl.ds(pl.multiple_of(a * K, K), K)
        t_nodes = [two_cols[start, q : q + 1] * 4.0 for q in range(3)]
        s_nodes = [
            jnp.concatenate([two_rows[index[q]], two_rows[index[q + 1]]], axis=1) * 4.0
            for q in range(0, len(index), 2)
        ]
        l_two[t] = couple(t_nodes, s_nodes, jnp.concatenate([m_two[q] for q in index], axis=0))
        return carry

    lax.fori_loop(0, coarse, level_two, 0)

    zero = jnp.zeros((K, R), BF16)

    def level_one(t, carry):
        index = [far_one[t, q] - group_base for q in range(far_one.shape[1])]
        start = pl.ds(pl.multiple_of(t * K, K), K)
        t_nodes = [own_nodes[start, q : q + 1] * 4.0 for q in range(3)]
        s_nodes = [
            jnp.concatenate([n_one[index[q]], n_one[index[q + 1]]], axis=1) for q in range(0, len(index), 2)
        ]
        g = couple(t_nodes, s_nodes, jnp.concatenate([m_one[q] for q in index], axis=0))
        chosen = l_two[uppers[t] - coarse_base]
        g = g + jnp.dot(lower[t], chosen, precision=HIGH, preferred_element_type=F32)
        high, low = split(g)
        g_left[t] = jnp.concatenate([high, zero, low, zero], axis=1)
        g_right[t] = jnp.concatenate([zero, high, zero, low], axis=1)
        return carry

    lax.fori_loop(0, boxes, level_one, 0)

    def pair(at):
        e_two = jnp.concatenate(split(transfer[:, pl.ds(pl.multiple_of(at * 2 * K, 2 * K), 2 * K)]), axis=0)
        p_zero = parents[at * 2] - box_base
        p_one = parents[at * 2 + 1] - box_base
        r = dot(e_two, jnp.concatenate([g_left[p_zero], g_right[p_one]], axis=0))
        g = r[:K, : 2 * R] + r[:K, 2 * R :] + r[K:, : 2 * R]
        turned = jnp.concatenate([g, g], axis=0).T
        high, low = split(turned)
        for side in range(2):
            c = at * 2 + side
            where = pl.ds(pl.multiple_of(c * B, B), B)
            b_two = jnp.concatenate(split(basis[:, where]), axis=0)
            rows = slice(side * R, (side + 1) * R)
            f = dot(jnp.concatenate([high[rows], low[rows]], axis=0), b_two)
            out[:, where] = masked(near[c] + (f[:R] + f[R:]), counts[c])

    group = 4

    def step(i, carry):
        for q in range(group):
            pair(i * group + q)
        return carry

    lax.fori_loop(0, near.shape[0] // 2 // group, step, 0)


def lists(slots, taken, counts):
    leaves = slots.shape[0]
    known = jnp.arange(counts.shape[0], dtype=jnp.int32)
    own = jnp.sum(jnp.where(slots[:, :, None] == known, counts, 0), axis=-1)
    blocks = jnp.where(taken, (own + ROWS - 1) // ROWS, 0)
    ends = jnp.sum(
        jnp.where(jnp.arange(NEAR)[:, None] >= jnp.arange(NEAR)[None, :], blocks[:, None, :], 0), axis=-1
    )
    starts = ends - blocks
    place = jnp.arange(SPAN, dtype=jnp.int32)
    inside = (place >= starts[:, :, None]) & (place < ends[:, :, None])
    null = counts.shape[0] * B
    base = (slots * B - starts * ROWS - null)[:, :, None]
    rows_of = null + jnp.sum(jnp.where(inside, base + place * ROWS, 0), axis=1)
    chunks = (ends[:, -1] + PER - 1) // PER
    leaf = jnp.arange(leaves, dtype=jnp.int32)
    after = jnp.sum(jnp.where(leaf[:, None] >= leaf[None, :], chunks[None, :], 0), axis=1)
    total = after[-1]
    t = jnp.arange(leaves * NEAR + UNROLL, dtype=jnp.int32)
    passed = t[:, None] >= after[None, :]
    at_leaf = jnp.sum(passed.astype(jnp.int32), axis=1)
    at_chunk = t - jnp.sum(jnp.where(passed, chunks[None, :], 0), axis=1)
    items = jnp.where(t < total, at_leaf * 16 + at_chunk, (leaves - 1) * 16 + NEAR)
    return items, rows_of, total.reshape(1)


def shifted(x, axis, by):
    count = lax.axis_size(axis)
    return lax.ppermute(x, axis, [(i, (i + by) % count) for i in range(count)])


def local(
    points,
    rhs,
    leaf_count,
    near_list,
    leaf_basis,
    leaf_transfer,
    leaf_parent,
    nodes1,
    box_transfer,
    box_parent,
    far1,
    nodes2,
    far2,
):
    leaves = leaf_count.shape[0]
    n_dev = lax.axis_size("dev")
    n_grp = lax.axis_size("grp")
    grp = lax.axis_index("grp")
    dev = lax.axis_index("dev")
    device = grp * n_dev + dev
    boxes = nodes1.shape[1] // K
    coarse = boxes * n_dev // CHILD
    width = REACH * B
    shape = jax.ShapeDtypeStruct

    up = [(i, i + 1) for i in range(n_dev - 1)]
    down = [(i + 1, i) for i in range(n_dev - 1)]
    both = jnp.concatenate([rhs, points], axis=0)
    before = lax.ppermute(both[:, -width:], "dev", up)
    after = lax.ppermute(both[:, :width], "dev", down)
    count_before = lax.ppermute(leaf_count[-REACH:], "dev", up)
    count_after = lax.ppermute(leaf_count[:REACH], "dev", down)
    halo_counts = jnp.concatenate([count_before, count_after])

    offset = jnp.stack([device * boxes, grp * coarse]).astype(jnp.int32)
    table, wanted, sent = pl.pallas_call(
        lambda *refs: upward(boxes, coarse, None, *refs),
        in_specs=[vmem()] * 6 + [smem()] * 4,
        out_specs=[vmem()] * 3,
        out_shape=[
            shape((leaves * B + ROWS, 2 * K), BF16),
            shape((leaves, K, B), BF16),
            shape((K + 8, (boxes + coarse) * R), F32),
        ],
        scratch_shapes=[
            pltpu.VMEM((boxes, R, 2 * K), F32),
            pltpu.VMEM((boxes, R, 2 * K), F32),
            pltpu.VMEM((coarse, R, K), F32),
        ],
        compiler_params=params(),
        name="upward",
    )(points, rhs, leaf_basis, leaf_transfer, nodes1, box_transfer, leaf_count, leaf_parent, box_parent, offset)

    all_sent = [sent] + [shifted(sent, "dev", k) for k in range(1, n_dev)]

    relative = near_list - device * leaves
    inside = (relative >= 0) & (relative < leaves)
    own_lists = lists(relative, inside, leaf_count)
    halo_slot = jnp.where(relative < 0, relative + REACH, relative - leaves + REACH)
    halo_lists = lists(halo_slot, ~inside, halo_counts)

    buffers = [pltpu.VMEM((B, 2 * K), BF16)] * UNROLL + [pltpu.VMEM((B, B), BF16)] * (2 * UNROLL)
    near = pl.pallas_call(
        near_own,
        in_specs=[smem()] * 3 + [vmem()] * 2,
        out_specs=vmem(),
        out_shape=shape((leaves, R, B), F32),
        scratch_shapes=buffers,
        compiler_params=params(),
        name="near_own",
    )(*own_lists, table, wanted)

    part = all_sent[0][:K, boxes * R :]
    for other in all_sent[1:]:
        part = part + other[:K, boxes * R :]
    tops = [part] + [shifted(part, "grp", k) for k in range(1, n_grp)]

    near = pl.pallas_call(
        near_halo,
        in_specs=[smem()] * 4 + [vmem()] * 4,
        out_specs=vmem(),
        out_shape=shape((leaves, R, B), F32),
        scratch_shapes=[pltpu.VMEM((2 * REACH * B + ROWS, 2 * K), BF16)] + buffers,
        compiler_params=params(),
        name="near_halo",
    )(*halo_lists, halo_counts, before, after, wanted, near)

    total_coarse = nodes2.shape[1] // K
    two_rows = jnp.pad(nodes2.reshape(3, total_coarse, K).transpose(1, 0, 2), ((0, 0), (0, 5), (0, 0)))
    where_am = jnp.stack([dev, grp, device * boxes, grp * coarse, grp * boxes * n_dev]).astype(jnp.int32)
    return pl.pallas_call(
        lambda *refs: downward(boxes, coarse, n_dev, n_grp, *refs),
        in_specs=[smem()] * 6 + [vmem()] * (n_dev + n_grp + 7),
        out_specs=vmem(),
        out_shape=shape((R, leaves * B), F32),
        scratch_shapes=[
            pltpu.VMEM((boxes * n_dev, K, 2 * R), BF16),
            pltpu.VMEM((total_coarse, K, 2 * R), BF16),
            pltpu.VMEM((boxes * n_dev, 8, K), F32),
            pltpu.VMEM((coarse, K, R), F32),
            pltpu.VMEM((boxes, K, 4 * R), BF16),
            pltpu.VMEM((boxes, K, 4 * R), BF16),
        ],
        compiler_params=params(),
        name="downward",
    )(
        far1,
        far2,
        leaf_count,
        leaf_parent,
        box_parent,
        where_am,
        *all_sent,
        *tops,
        leaf_basis,
        leaf_transfer,
        box_transfer.reshape(K, boxes, K).transpose(1, 0, 2),
        nodes1.T,
        two_rows,
        nodes2.T,
        near,
    )


def solution(mesh):
    placed = (
        P(None, ("grp", "dev")),
        P(None, ("grp", "dev")),
        P(("grp", "dev")),
        P(("grp", "dev"), None),
        P(None, ("grp", "dev")),
        P(None, ("grp", "dev")),
        P(("grp", "dev")),
        P(None, ("grp", "dev")),
        P(None, ("grp", "dev")),
        P(("grp", "dev")),
        P(("grp", "dev"), None),
        P(),
        P(),
    )
    return jax.shard_map(
        local, mesh=mesh, in_specs=placed, out_specs=P(None, ("grp", "dev")), check_vma=False
    )
```

```python
import jax
import jax.numpy as jnp
from jax import lax
from jax.experimental import pallas as pl
from jax.experimental.pallas import tpu as pltpu
from jax.sharding import PartitionSpec as P

B = 256
K = 64
R = 32
NEAR = 8
CHILD = 8
REACH = 32
ROWS = 16
PER = B // ROWS
UNROLL = 8
SPAN = NEAR * PER + PER

F32 = jnp.float32
BF16 = jnp.bfloat16
LIMIT = 58 * 1024 * 1024

PIECES = ((0, 0), (0, 1), (1, 0), (1, 1), (0, 2), (2, 0), (1, 2), (2, 1))


def params():
    return pltpu.CompilerParams(vmem_limit_bytes=LIMIT)


def cost(us):
    return pl.CostEstimate(flops=us * 10**9, bytes_accessed=us * 3 * 10**6, transcendentals=0)


def vmem():
    return pl.BlockSpec(memory_space=pltpu.VMEM)


def smem():
    return pl.BlockSpec(memory_space=pltpu.SMEM)


def split(x):
    high = x.astype(BF16)
    return high, (x - high.astype(F32)).astype(BF16)


def to_grid(x, step):
    big = 1.5 * 2.0**23 * step
    return (x + big) - big


def dot(a, b):
    return jnp.dot(a, b, preferred_element_type=F32)


def dot_nt(a, b):
    return lax.dot_general(a, b, (((1,), (1,)), ((), ())), preferred_element_type=F32)


def features(coords, targets=True):
    n = coords.shape[1]
    scaled = jnp.concatenate([coords * 4.0, jnp.zeros((5, n), F32)], axis=0)
    one = to_grid(scaled, 2.0**-3)
    rest = scaled - one
    two = to_grid(rest, 2.0**-11)
    three = rest - two
    pieces = (one, two, three)
    square = jnp.sum(one * one, axis=0, keepdims=True)
    s_one = to_grid(square, 8.0)
    s_two = square - s_one
    tail = jnp.sum(rest * (scaled + one), axis=0, keepdims=True)
    q_one = to_grid(tail, 2.0**-4)
    tail = tail - q_one
    q_two = to_grid(tail, 2.0**-12)
    norms = (s_one, s_two, q_one, q_two, tail - q_two)
    row = lax.broadcasted_iota(jnp.int32, (8, n), 0)
    sources, wanted = [], []
    for at, (first, second) in enumerate(PIECES):
        src = pieces[first]
        tgt = pieces[second] * -2.0
        if at < 5:
            src = jnp.where(row == 3, norms[at], jnp.where(row == 4, 1.0, src))
            tgt = jnp.where(row == 3, 1.0, jnp.where(row == 4, norms[at], tgt))
        elif at == 5:
            src = jnp.where(row == 3, 1.0, src)
            tgt = jnp.where(row == 3, 1.0, tgt)
        sources.append(src)
        wanted.append(tgt)
    source = jnp.concatenate(sources, axis=0).astype(BF16)
    if not targets:
        return source, None
    return source, jnp.concatenate(wanted, axis=0).astype(BF16)


def masked(x, count):
    slot = lax.broadcasted_iota(jnp.int32, x.shape, 1)
    return jnp.where(slot < count, x, 0.0)


def lists(slots, taken, counts, null):
    leaves = slots.shape[0]
    lane = lax.broadcasted_iota(jnp.int32, (leaves, counts.shape[1]), 1)
    place = lax.broadcasted_iota(jnp.int32, (leaves, SPAN), 1)
    rows_of = jnp.full((leaves, SPAN), null, jnp.int32)
    start = jnp.zeros((leaves, 1), jnp.int32)
    for e in range(NEAR):
        slot = slots[:, e : e + 1]
        count = jnp.sum(jnp.where(slot == lane, counts, 0.0), axis=1, keepdims=True).astype(jnp.int32)
        end = start + jnp.where(taken[:, e : e + 1], (count + ROWS - 1) // ROWS, 0)
        rows_of = jnp.where((place >= start) & (place < end), slot * B + (place - start) * ROWS, rows_of)
        start = end
    chunks = ((start + PER - 1) // PER).astype(F32)
    below = lax.broadcasted_iota(jnp.int32, (leaves, leaves), 0) >= lax.broadcasted_iota(
        jnp.int32, (leaves, leaves), 1
    )
    after = dot(below.astype(F32).astype(BF16), jnp.broadcast_to(chunks, (leaves, 128)).astype(BF16))
    width = -(-(leaves * NEAR + UNROLL) // 128) * 128
    t = lax.broadcasted_iota(jnp.int32, (leaves, width), 1).astype(F32)
    passed = t >= after[:, :1]
    at_leaf = jnp.sum(jnp.where(passed, 1.0, 0.0), axis=0, keepdims=True)
    at_chunk = t[:1] - jnp.sum(jnp.where(passed, chunks, 0.0), axis=0, keepdims=True)
    total = jnp.broadcast_to(after[leaves - 1 :, :1], (1, width))
    items = jnp.where(t[:1] < total, at_leaf * 16.0 + at_chunk, (leaves - 1) * 16.0 + NEAR)
    row = lax.broadcasted_iota(jnp.int32, (8, width), 0)
    return jnp.where(row == 0, items, total).astype(jnp.int32), rows_of


def upward(boxes, coarse, leaves, points, rhs, basis, transfer, nodes, lower, near, row_counts, counts, parents, uppers, offset, table, wanted, sent, items, rows_of, left, right, top):
    at_step = pl.program_id(0)
    group = wanted.shape[0]

    @pl.when(at_step == 0)
    def _():
        left[...] = jnp.zeros_like(left)
        right[...] = jnp.zeros_like(right)
        top[...] = jnp.zeros_like(top)
        slots = near[...] - offset[2]
        items[...], rows_of[...] = lists(slots, (slots >= 0) & (slots < leaves), row_counts[...].astype(F32), leaves * B)

    def pair(at):
        rows = []
        first = at_step * group + at * 2
        for side in range(2):
            c = at * 2 + side
            where = slice(c * B, (c + 1) * B)
            x = masked(rhs[:, where], counts[first + side])
            x_two = jnp.concatenate(split(x), axis=0)
            source, target = features(points[:, where])
            wanted[c] = target
            table[where, :] = jnp.concatenate([source, x_two], axis=0).T
            b_two = jnp.concatenate(split(basis[:, where]), axis=0)
            r = dot_nt(x_two, b_two)
            rows.append(r[:R, :K] + r[:R, K:] + r[R:, :K])
        m = jnp.concatenate(rows, axis=0)
        high, low = split(m)
        left_side = jnp.concatenate(
            [jnp.concatenate([high, high], axis=1), jnp.concatenate([low, low], axis=1)], axis=0
        )
        e_two = jnp.concatenate(split(transfer[:, at * 2 * K : (at + 1) * 2 * K]), axis=0)
        lifted = dot(left_side, e_two)
        lifted = lifted[: 2 * R] + lifted[2 * R :]
        left[parents[first] - offset[0]] += lifted[:R]
        right[parents[first + 1] - offset[0]] += lifted[R:]

    @pl.when(at_step * group < leaves)
    def _():
        for at in range(group // 2):
            pair(at)

    @pl.when(at_step * group >= leaves)
    def _():
        source, _ = features(jnp.zeros((3, B), F32), False)
        rows = jnp.concatenate([source, jnp.zeros((2 * R, B), BF16)], axis=0).T
        table[:B, :] = rows
        m_one = [left[b][:, :K] + right[b][:, K:] for b in range(boxes)]
        for b in range(boxes):
            f = lower[:, (b // 2) * 2 * K : (b // 2 + 1) * 2 * K]
            f_two = jnp.concatenate(split(f), axis=0)
            high, low = split(m_one[b])
            raised = dot(
                jnp.concatenate(
                    [jnp.concatenate([high, high], axis=1), jnp.concatenate([low, low], axis=1)], axis=0
                ),
                f_two,
            )
            raised = raised[:R] + raised[R:]
            top[uppers[b] - offset[1]] += raised[:, (b % 2) * K : (b % 2 + 1) * K]
        sent[K : K + 8, :] = jnp.zeros((8, sent.shape[1]), F32)
        sent[K : K + 3, : boxes * K] = nodes[...]
        for q in range(boxes // 4):
            block = jnp.concatenate(m_one[4 * q : 4 * q + 4], axis=0)
            sent[:K, q * 4 * R : (q + 1) * 4 * R] = block.T
        for q in range(coarse // 4):
            block = jnp.concatenate([top[4 * q + z] for z in range(4)], axis=0)
            sent[:K, (boxes + 4 * q) * R : (boxes + 4 * q + 4) * R] = block.T


def near_items(items, rows_of, table, wanted, out, kept, highs, lows):
    def first(t, s):
        code = items[0, t]
        c = code // 16
        base = (code % 16) * PER
        rows = jnp.concatenate(
            [table[pl.ds(pl.multiple_of(rows_of[c, base + q], ROWS), ROWS), :] for q in range(PER)], axis=0
        )
        kept[s][...] = rows
        u = dot(rows[:, :K], wanted[c])
        high, low = split(lax.rsqrt(u))
        highs[s][...] = high
        lows[s][...] = low

    def second(t, s):
        c = items[0, t] // 16
        x = kept[s][...].T[K:]
        a = dot(x, highs[s][...])
        b = dot(x[:R], lows[s][...])
        out[c] += a[:R] + a[R:] + b

    groups = (items[1, 0] + UNROLL - 1) // UNROLL

    @pl.when(groups > 0)
    def _():
        for q in range(UNROLL):
            first(q, q)

        def step(g, carry):
            for q in range(UNROLL):
                second((g - 1) * UNROLL + q, q)
                first(g * UNROLL + q, q)
            return carry

        lax.fori_loop(1, groups, step, 0)
        for q in range(UNROLL):
            second((groups - 1) * UNROLL + q, q)


def near_own(items, rows_of, table, wanted, out, *scratch):
    kept, highs, lows = scratch[:UNROLL], scratch[UNROLL : 2 * UNROLL], scratch[2 * UNROLL :]
    out[...] = jnp.zeros_like(out)
    near_items(items, rows_of, table, wanted, out, kept, highs, lows)


def halo_table(leaves, before, after, near, offset, table, items, rows_of, counts):
    at_step = pl.program_id(0)
    group = before.shape[1] // B
    side = table.shape[0] // 2 // B
    steps = REACH // group
    lane = lax.broadcasted_iota(jnp.int32, counts.shape, 1)

    @pl.when(at_step == 0)
    def _():
        counts[...] = jnp.zeros_like(counts)

    @pl.when(at_step < steps)
    def _():
        for part, data in ((0, before), (1, after)):
            for q in range(group):
                where = slice(q * B, (q + 1) * B)
                count = data[R + 3 : R + 4, where]
                slot = lax.broadcasted_iota(jnp.int32, (R, B), 1).astype(F32)
                x = jnp.where(slot < count, data[:R, where], 0.0)
                source, _ = features(data[R : R + 3, where], False)
                to = slice((part * side + q) * B, (part * side + q + 1) * B)
                table[to, :] = jnp.concatenate([source, *split(x)], axis=0).T
                slot = (at_step * 2 + part) * group + q
                counts[...] = jnp.where(lane == slot, count[:, :1], counts[...])

    @pl.when(at_step == steps)
    def _():
        source, _ = features(jnp.zeros((3, B), F32), False)
        table[:B, :] = jnp.concatenate([source, jnp.zeros((2 * R, B), BF16)], axis=0).T
        relative = near[...] - offset[2]
        taken = (relative < 0) | (relative >= leaves)
        h = jnp.where(relative < 0, relative + REACH, relative - leaves)
        slots = (h // group * 2 + jnp.where(relative < 0, 0, 1)) * group + h % group
        items[...], rows_of[...] = lists(slots, taken, counts[:1, : 2 * REACH], 2 * REACH * B)


def near_halo(items, rows_of, table, wanted, begun, out, *scratch):
    kept, highs, lows = scratch[:UNROLL], scratch[UNROLL : 2 * UNROLL], scratch[2 * UNROLL :]
    out[...] = begun[...]
    near_items(items, rows_of, table, wanted, out, kept, highs, lows)


def couple(t_nodes, s_nodes, expansions):
    tiles = []
    for s in s_nodes:
        d = [t_nodes[q] - s[q : q + 1] for q in range(3)]
        tiles.append(lax.rsqrt(1.0 + (d[0] * d[0] + d[1] * d[1] + d[2] * d[2])))
    high, low = split(jnp.concatenate(tiles, axis=1))
    r = dot(jnp.concatenate([high, low], axis=0), expansions)
    return r[:K, :R] + r[:K, R:] + r[K:, :R]


def columns(nodes):
    padded = jnp.concatenate([nodes * 4.0, jnp.zeros((5, nodes.shape[1]), F32)], axis=0)
    return padded.T


def downward(boxes, coarse, n_dev, n_grp, far_one, far_two, counts, parents, uppers, where_am, *refs):
    sent = refs[:n_dev]
    tops = refs[n_dev : n_dev + n_grp]
    basis, transfer, lower, nodes_one, nodes_two, near, out = refs[n_dev + n_grp : n_dev + n_grp + 7]
    m_one, m_two, n_one, n_two, c_one, c_two, l_two, g_left, g_right = refs[n_dev + n_grp + 7 :]
    dev, grp, box_base, coarse_base, group_base = [where_am[q] for q in range(5)]

    @pl.when(pl.program_id(0) == 0)
    def _():
        for k in range(n_dev):
            at = lax.rem(dev - k + n_dev, n_dev)
            data = sent[k]
            for b in range(boxes):
                m_one[at * boxes + b] = jnp.concatenate(split(data[:K, b * R : (b + 1) * R]), axis=1)
                n_one[at * boxes + b] = data[K : K + 8, b * K : (b + 1) * K] * 4.0
        for k in range(n_grp):
            at = lax.rem(grp - k + n_grp, n_grp)
            data = tops[k]
            for b in range(coarse):
                m_two[at * coarse + b] = jnp.concatenate(split(data[:, b * R : (b + 1) * R]), axis=1)
        for b in range(n_grp * coarse):
            n_two[b, :3] = nodes_two[:, b * K : (b + 1) * K] * 4.0
        c_one[...] = columns(nodes_one[...])
        c_two[...] = columns(nodes_two[...])

        def tiles(nodes, index):
            return [
                jnp.concatenate([nodes[index[q]], nodes[index[q + 1]]], axis=1) for q in range(0, len(index), 2)
            ]

        for t in range(coarse):
            a = coarse_base + t
            index = [far_two[a, q] for q in range(far_two.shape[1])]
            start = pl.ds(pl.multiple_of(a * K, K), K)
            t_nodes = [c_two[start, q : q + 1] for q in range(3)]
            l_two[t] = couple(t_nodes, tiles(n_two, index), jnp.concatenate([m_two[q] for q in index], axis=0))

        zero = jnp.zeros((K, R), BF16)
        for t in range(boxes):
            index = [far_one[t, q] - group_base for q in range(far_one.shape[1])]
            t_nodes = [c_one[t * K : (t + 1) * K, q : q + 1] for q in range(3)]
            g = couple(t_nodes, tiles(n_one, index), jnp.concatenate([m_one[q] for q in index], axis=0))
            chosen = jnp.concatenate(split(l_two[uppers[t] - coarse_base]), axis=1)
            f_two = jnp.concatenate(split(lower[:, t * K : (t + 1) * K]), axis=0)
            r = dot(f_two, chosen)
            g = g + (r[:K, :R] + r[:K, R:] + r[K:, :R])
            high, low = split(g)
            g_left[t] = jnp.concatenate([high, zero, low, zero], axis=1)
            g_right[t] = jnp.concatenate([zero, high, zero, low], axis=1)

    group = near.shape[0]
    for at in range(group // 2):
        e_two = jnp.concatenate(split(transfer[:, at * 2 * K : (at + 1) * 2 * K]), axis=0)
        first = pl.program_id(0) * group + at * 2
        p_zero = parents[first] - box_base
        p_one = parents[first + 1] - box_base
        r = dot(e_two, jnp.concatenate([g_left[p_zero], g_right[p_one]], axis=0))
        g = r[:K, : 2 * R] + r[:K, 2 * R :] + r[K:, : 2 * R]
        turned = jnp.concatenate([g, g], axis=0).T
        high, low = split(turned)
        for side in range(2):
            c = at * 2 + side
            where = slice(c * B, (c + 1) * B)
            b_two = jnp.concatenate(split(basis[:, where]), axis=0)
            rows = slice(side * R, (side + 1) * R)
            f = dot(jnp.concatenate([high[rows], low[rows]], axis=0), b_two)
            out[:, where] = masked(near[c] + (f[:R] + f[R:]), counts[first + side])


def shifted(x, axis, by):
    count = lax.axis_size(axis)
    return lax.ppermute(x, axis, [(i, (i + by) % count) for i in range(count)])


def local(
    points,
    rhs,
    leaf_count,
    near_list,
    leaf_basis,
    leaf_transfer,
    leaf_parent,
    nodes1,
    box_transfer,
    box_parent,
    far1,
    nodes2,
    far2,
):
    leaves = leaf_count.shape[0]
    n_dev = lax.axis_size("dev")
    n_grp = lax.axis_size("grp")
    grp = lax.axis_index("grp")
    dev = lax.axis_index("dev")
    device = grp * n_dev + dev
    boxes = nodes1.shape[1] // K
    coarse = boxes * n_dev // CHILD
    width = REACH * B
    shape = jax.ShapeDtypeStruct

    up = [(i, i + 1) for i in range(n_dev - 1)]
    down = [(i + 1, i) for i in range(n_dev - 1)]

    def packed(side, some):
        count = jnp.broadcast_to(some.astype(F32)[:, None], (REACH, B)).reshape(1, width)
        return jnp.concatenate([rhs[:, side], points[:, side], count], axis=0)

    before = lax.ppermute(packed(slice(leaves * B - width, leaves * B), leaf_count[-REACH:]), "dev", up)
    after = lax.ppermute(packed(slice(0, width), leaf_count[:REACH]), "dev", down)

    where_am = jnp.stack([device * boxes, grp * coarse, device * leaves, dev, grp, grp * boxes * n_dev]).astype(
        jnp.int32
    )
    group = 8
    steps = leaves // group
    last = steps - 1
    table_rows = (leaves + group) * B
    listed = [
        shape((8, -(-(leaves * NEAR + UNROLL) // 128) * 128), jnp.int32),
        shape((leaves, SPAN), jnp.int32),
    ]

    def along(rows, size):
        return pl.BlockSpec((rows, size), lambda i: (0, jnp.minimum(i, last)))

    def down_rows(dims):
        return pl.BlockSpec((group, *dims), lambda i: (jnp.minimum(i, last), 0, 0))

    def whole(dims):
        return pl.BlockSpec(dims, lambda i: (0,) * len(dims))

    table, wanted, sent, *own_lists = pl.pallas_call(
        lambda *refs: upward(boxes, coarse, leaves, *refs),
        grid=(steps + 1,),
        in_specs=[
            along(3, group * B),
            along(R, group * B),
            along(K, group * B),
            along(K, group * K),
            whole(nodes1.shape),
            whole(box_transfer.shape),
            whole(near_list.shape),
            whole((1, leaves)),
        ]
        + [smem()] * 4,
        out_specs=[
            pl.BlockSpec((group * B, 2 * K), lambda i: (i, 0)),
            down_rows((K, B)),
            whole((K + 8, (boxes + coarse) * R)),
            whole(listed[0].shape),
            whole(listed[1].shape),
        ],
        out_shape=[
            shape((table_rows, 2 * K), BF16),
            shape((leaves, K, B), BF16),
            shape((K + 8, (boxes + coarse) * R), F32),
            *listed,
        ],
        scratch_shapes=[
            pltpu.VMEM((boxes, R, 2 * K), F32),
            pltpu.VMEM((boxes, R, 2 * K), F32),
            pltpu.VMEM((coarse, R, K), F32),
        ],
        compiler_params=params(),
        cost_estimate=cost(14),
        name="upward",
    )(
        points,
        rhs,
        leaf_basis,
        leaf_transfer,
        nodes1,
        box_transfer,
        near_list,
        leaf_count.reshape(1, leaves),
        leaf_count,
        leaf_parent,
        box_parent,
        where_am,
    )

    all_sent = [sent] + [shifted(sent, "dev", k) for k in range(1, n_dev)]

    buffers = [pltpu.VMEM((B, 2 * K), BF16)] * UNROLL + [pltpu.VMEM((B, B), BF16)] * (2 * UNROLL)
    near = pl.pallas_call(
        near_own,
        in_specs=[smem()] * 2 + [vmem()] * 2,
        out_specs=vmem(),
        out_shape=shape((leaves, R, B), F32),
        scratch_shapes=buffers,
        compiler_params=params(),
        cost_estimate=cost(32),
        name="near_own",
    )(*own_lists, table, wanted)

    part = all_sent[0][:K, boxes * R :]
    for other in all_sent[1:]:
        part = part + other[:K, boxes * R :]
    part, near = lax.optimization_barrier((part, near))
    tops = [part] + [shifted(part, "grp", k) for k in range(1, n_grp)]

    half = REACH // (group // 2)

    def piece(i):
        return (0, jnp.minimum(i, half - 1))

    outer, *halo_lists = pl.pallas_call(
        lambda *refs: halo_table(leaves, *refs),
        grid=(half + 1,),
        in_specs=[
            pl.BlockSpec((R + 4, group // 2 * B), piece),
            pl.BlockSpec((R + 4, group // 2 * B), piece),
            whole(near_list.shape),
            smem(),
        ],
        out_specs=[
            pl.BlockSpec((group * B, 2 * K), lambda i: (i, 0)),
            whole(listed[0].shape),
            whole(listed[1].shape),
        ],
        out_shape=[shape(((2 * REACH + group) * B, 2 * K), BF16), *listed],
        scratch_shapes=[pltpu.VMEM((8, 128), F32)],
        compiler_params=params(),
        cost_estimate=cost(5),
        name="halo_table",
    )(before, after, near_list, where_am)

    near = pl.pallas_call(
        near_halo,
        in_specs=[smem()] * 2 + [vmem()] * 3,
        out_specs=vmem(),
        out_shape=shape((leaves, R, B), F32),
        scratch_shapes=buffers,
        compiler_params=params(),
        cost_estimate=cost(12),
        name="near_halo",
    )(*halo_lists, outer, wanted, near)

    total_coarse = nodes2.shape[1] // K
    scalars = jnp.stack([where_am[q] for q in (3, 4, 0, 1, 5)])
    return pl.pallas_call(
        lambda *refs: downward(boxes, coarse, n_dev, n_grp, *refs),
        grid=(steps,),
        in_specs=[smem()] * 6
        + [whole(sent.shape)] * n_dev
        + [whole(part.shape)] * n_grp
        + [
            along(K, group * B),
            along(K, group * K),
            whole(box_transfer.shape),
            whole(nodes1.shape),
            whole(nodes2.shape),
            down_rows((R, B)),
        ],
        out_specs=along(R, group * B),
        out_shape=shape((R, leaves * B), F32),
        scratch_shapes=[
            pltpu.VMEM((boxes * n_dev, K, 2 * R), BF16),
            pltpu.VMEM((total_coarse, K, 2 * R), BF16),
            pltpu.VMEM((boxes * n_dev, 8, K), F32),
            pltpu.VMEM((total_coarse, 8, K), F32),
            pltpu.VMEM((boxes * K, 8), F32),
            pltpu.VMEM((total_coarse * K, 8), F32),
            pltpu.VMEM((coarse, K, R), F32),
            pltpu.VMEM((boxes, K, 4 * R), BF16),
            pltpu.VMEM((boxes, K, 4 * R), BF16),
        ],
        compiler_params=params(),
        cost_estimate=cost(15),
        name="downward",
    )(
        far1,
        far2,
        leaf_count,
        leaf_parent,
        box_parent,
        scalars,
        *all_sent,
        *tops,
        leaf_basis,
        leaf_transfer,
        box_transfer,
        nodes1,
        nodes2,
        near,
    )


def solution(mesh):
    placed = (
        P(None, ("grp", "dev")),
        P(None, ("grp", "dev")),
        P(("grp", "dev")),
        P(("grp", "dev"), None),
        P(None, ("grp", "dev")),
        P(None, ("grp", "dev")),
        P(("grp", "dev")),
        P(None, ("grp", "dev")),
        P(None, ("grp", "dev")),
        P(("grp", "dev")),
        P(("grp", "dev"), None),
        P(),
        P(),
    )
    return jax.shard_map(
        local, mesh=mesh, in_specs=placed, out_specs=P(None, ("grp", "dev")), check_vma=False
    )
```

```python
import jax
import jax.numpy as jnp
from jax import lax
from jax.experimental import pallas as pl
from jax.experimental.pallas import tpu as pltpu
from jax.sharding import PartitionSpec as P

B = 256
K = 64
R = 32
NEAR = 8
CHILD = 8
REACH = 32
FAR1 = 16
FAR2 = 8
ROWS = 16
PER = B // ROWS
UNROLL = 8
GROUP = 16
SPAN = NEAR * PER + PER

F32 = jnp.float32
BF16 = jnp.bfloat16
LIMIT = 20 * 1024 * 1024
LARGE = 58 * 1024 * 1024

PIECES = ((0, 0), (0, 1), (1, 0), (1, 1), (0, 2), (2, 0), (1, 2), (2, 1))


def params(limit=LIMIT):
    return pltpu.CompilerParams(vmem_limit_bytes=limit)


class Part:
    def __init__(self, ref, base, cols=1):
        self.ref, self.base, self.cols = ref, base, cols

    def __getitem__(self, at):
        if isinstance(at, tuple):
            return self.ref[self.base + at[0] * self.cols + at[1]]
        return self.ref[self.base + at]


def parts(ref, leaves, boxes):
    sizes = (leaves, leaves, boxes, 6, boxes * FAR1)
    bases = [sum(sizes[:q]) for q in range(6)]
    return [Part(ref, base, cols) for base, cols in zip(bases, (1, 1, 1, 1, FAR1, FAR2))]


def cost(us):
    return pl.CostEstimate(flops=us * 10**9, bytes_accessed=us * 3 * 10**6, transcendentals=0)


def vmem():
    return pl.BlockSpec(memory_space=pltpu.VMEM)


def smem():
    return pl.BlockSpec(memory_space=pltpu.SMEM)


def split(x):
    high = x.astype(BF16)
    return high, (x - high.astype(F32)).astype(BF16)


def to_grid(x, step):
    big = 1.5 * 2.0**23 * step
    return (x + big) - big


def dot(a, b):
    return jnp.dot(a, b, preferred_element_type=F32)


def dot_nt(a, b):
    return lax.dot_general(a, b, (((1,), (1,)), ((), ())), preferred_element_type=F32)


def features(coords, targets=True):
    n = coords.shape[1]
    scaled = jnp.concatenate([coords * 4.0, jnp.zeros((5, n), F32)], axis=0)
    one = to_grid(scaled, 2.0**-3)
    rest = scaled - one
    two = to_grid(rest, 2.0**-11)
    three = rest - two
    pieces = (one, two, three)
    square = jnp.sum(one * one, axis=0, keepdims=True)
    s_one = to_grid(square, 8.0)
    s_two = square - s_one
    tail = jnp.sum(rest * (scaled + one), axis=0, keepdims=True)
    q_one = to_grid(tail, 2.0**-4)
    tail = tail - q_one
    q_two = to_grid(tail, 2.0**-12)
    norms = (s_one, s_two, q_one, q_two, tail - q_two)
    row = lax.broadcasted_iota(jnp.int32, (8, n), 0)
    sources, wanted = [], []
    for at, (first, second) in enumerate(PIECES):
        src = pieces[first]
        tgt = pieces[second] * -2.0
        if at < 5:
            src = jnp.where(row == 3, norms[at], jnp.where(row == 4, 1.0, src))
            tgt = jnp.where(row == 3, 1.0, jnp.where(row == 4, norms[at], tgt))
        elif at == 5:
            src = jnp.where(row == 3, 1.0, src)
            tgt = jnp.where(row == 3, 1.0, tgt)
        sources.append(src)
        wanted.append(tgt)
    source = jnp.concatenate(sources, axis=0).astype(BF16)
    if not targets:
        return source, None
    return source, jnp.concatenate(wanted, axis=0).astype(BF16)


def masked(x, count):
    slot = lax.broadcasted_iota(jnp.int32, x.shape, 1)
    return jnp.where(slot < count, x, 0.0)


def lists(slots, taken, counts, null):
    leaves = slots.shape[0]
    lane = lax.broadcasted_iota(jnp.int32, (leaves, counts.shape[1]), 1)
    place = lax.broadcasted_iota(jnp.int32, (leaves, SPAN), 1)
    rows_of = jnp.full((leaves, SPAN), null, jnp.int32)
    start = jnp.zeros((leaves, 1), jnp.int32)
    for e in range(NEAR):
        slot = slots[:, e : e + 1]
        count = jnp.sum(jnp.where(slot == lane, counts, 0.0), axis=1, keepdims=True).astype(jnp.int32)
        end = start + jnp.where(taken[:, e : e + 1], (count + ROWS - 1) >> 4, 0)
        rows_of = jnp.where((place >= start) & (place < end), slot * B + (place - start) * ROWS, rows_of)
        start = end
    chunks = ((start + PER - 1) >> 4).astype(F32)
    below = lax.broadcasted_iota(jnp.int32, (leaves, leaves), 0) >= lax.broadcasted_iota(
        jnp.int32, (leaves, leaves), 1
    )
    after = dot(below.astype(F32).astype(BF16), jnp.broadcast_to(chunks, (leaves, 128)).astype(BF16))
    width = -(-(leaves * NEAR + UNROLL) // 128) * 128
    t = lax.broadcasted_iota(jnp.int32, (leaves, width), 1).astype(F32)
    passed = t >= after[:, :1]
    at_leaf = jnp.sum(jnp.where(passed, 1.0, 0.0), axis=0, keepdims=True)
    at_chunk = t[:1] - jnp.sum(jnp.where(passed, chunks, 0.0), axis=0, keepdims=True)
    total = jnp.broadcast_to(after[leaves - 1 :, :1], (1, width))
    items = jnp.where(t[:1] < total, at_leaf * 16.0 + at_chunk, (leaves - 1) * 16.0 + NEAR)
    row = lax.broadcasted_iota(jnp.int32, (8, width), 0)
    return jnp.where(row == 0, items, total).astype(jnp.int32), rows_of


def pack(far_rhs, points, first, last, sems):
    width = first.shape[1]
    leaves_end = far_rhs.shape[1]
    made = []
    for q, (out, start) in enumerate(((first, 0), (last, leaves_end - width))):
        made.append(pltpu.make_async_copy(far_rhs.at[:, start : start + width], out.at[:R, :], sems.at[q]))
        made[-1].start()
    for out, start in ((first, 0), (last, leaves_end - width)):
        out[R : R + 3, :] = points[:, start : start + width]
    for copy in made:
        copy.wait()


def null_rows(table, start):
    source, _ = features(jnp.zeros((3, B), F32), False)
    rows = jnp.concatenate([source, jnp.zeros((2 * R, B), BF16)], axis=0).T
    table[start : start + ROWS, :] = rows[:ROWS, :]


def copies(pairs, sems, i, size):
    made = []
    for q, (src, dst, per) in enumerate(pairs):
        where = pl.ds(pl.multiple_of(i * size * per, size * per), size * per)
        made.append(pltpu.make_async_copy(src.at[:, where], dst.at[:, where], sems.at[i, q]))
    return made


def upward(boxes, coarse, leaves, far_rhs, far_basis, far_transfer, nodes, lower, row_counts, scalars, sent, left, right, top, rhs, basis, transfer, moments, sems):
    counts, parents, uppers, offset, _, _ = parts(scalars, leaves, boxes)
    pairs = ((far_rhs, rhs, B), (far_basis, basis, B), (far_transfer, transfer, K))
    steps = leaves // GROUP
    for i in range(steps):
        for copy in copies(pairs, sems, i, GROUP):
            copy.start()
    left[...] = jnp.zeros_like(left)
    right[...] = jnp.zeros_like(right)
    top[...] = jnp.zeros_like(top)

    def gather(c):
        where = pl.ds(pl.multiple_of(c * B, B), B)
        x_two = jnp.concatenate(split(masked(rhs[:, where], counts[c])), axis=0)
        r = dot_nt(x_two, jnp.concatenate(split(basis[:, where]), axis=0))
        moments[c] = r[:R, :K] + r[:R, K:] + r[R:, :K]

    def lift(at):
        first = at * 2
        high, low = split(jnp.concatenate([moments[first], moments[first + 1]], axis=0))
        left_side = jnp.concatenate(
            [jnp.concatenate([high, high], axis=1), jnp.concatenate([low, low], axis=1)], axis=0
        )
        e_two = jnp.concatenate(split(transfer[:, pl.ds(pl.multiple_of(at * 2 * K, 2 * K), 2 * K)]), axis=0)
        lifted = dot(left_side, e_two)
        lifted = lifted[: 2 * R] + lifted[2 * R :]
        left[parents[first] - offset[0]] += lifted[:R]
        right[parents[first + 1] - offset[0]] += lifted[R:]

    def step(i, carry):
        for copy in copies(pairs, sems, i, GROUP):
            copy.wait()
        for q in range(GROUP):
            gather(i * GROUP + q)
        return carry

    def second(i, carry):
        for q in range(GROUP // 2):
            lift(i * (GROUP // 2) + q)
        return carry

    lax.fori_loop(0, steps, step, 0)
    lax.fori_loop(0, steps, second, 0)
    m_one = [left[b][:, :K] + right[b][:, K:] for b in range(boxes)]
    for b in range(boxes):
        f = lower[:, (b // 2) * 2 * K : (b // 2 + 1) * 2 * K]
        f_two = jnp.concatenate(split(f), axis=0)
        high, low = split(m_one[b])
        raised = dot(
            jnp.concatenate(
                [jnp.concatenate([high, high], axis=1), jnp.concatenate([low, low], axis=1)], axis=0
            ),
            f_two,
        )
        raised = raised[:R] + raised[R:]
        top[uppers[b] - offset[1]] += raised[:, (b % 2) * K : (b % 2 + 1) * K]
    sent[K : K + 8, :] = jnp.zeros((8, sent.shape[1]), F32)
    sent[K : K + 3, : boxes * K] = nodes[...]
    sent[K + 3 : K + 4, :leaves] = row_counts[...].astype(F32)
    for q in range(boxes // 4):
        block = jnp.concatenate(m_one[4 * q : 4 * q + 4], axis=0)
        sent[:K, q * 4 * R : (q + 1) * 4 * R] = block.T
    for q in range(coarse // 4):
        block = jnp.concatenate([top[4 * q + z] for z in range(4)], axis=0)
        sent[:K, (boxes + 4 * q) * R : (boxes + 4 * q + 4) * R] = block.T


def near_items(items, rows_of, table, wanted, out, kept, highs, lows):
    def first(t, s):
        code = items[0, t]
        c = code >> 4
        base = (code & 15) * PER
        rows = jnp.concatenate(
            [table[pl.ds(pl.multiple_of(rows_of[c, base + q], ROWS), ROWS), :] for q in range(PER)], axis=0
        )
        kept[s][...] = rows
        u = dot(rows[:, :K], wanted[c])
        high, low = split(lax.rsqrt(u))
        highs[s][...] = high
        lows[s][...] = low

    def second(t, s):
        c = items[0, t] >> 4
        x = kept[s][...].T[K:]
        a = dot(x, highs[s][...])
        b = dot(x[:R], lows[s][...])
        out[c] += a[:R] + a[R:] + b

    groups = lax.div(items[1, 0] + (UNROLL - 1), UNROLL)

    @pl.when(groups > 0)
    def _():
        for q in range(UNROLL):
            first(q, q)

        def step(g, carry):
            for q in range(UNROLL):
                second((g - 1) * UNROLL + q, q)
                first(g * UNROLL + q, q)
            return carry

        lax.fori_loop(1, groups, step, 0)
        for q in range(UNROLL):
            second((groups - 1) * UNROLL + q, q)


def own_table(leaves, far_points, far_rhs, near, row_counts, counts, offset, wanted, items, rows_of, tick, table, points, rhs, sems):
    pairs = ((far_points, points, B), (far_rhs, rhs, B))
    steps = leaves // GROUP
    for i in range(steps):
        for copy in copies(pairs, sems, i, GROUP):
            copy.start()
    tick[...] = jnp.zeros_like(tick)
    slots = near[...] - offset[2]
    items[...], rows_of[...] = lists(slots, (slots >= 0) & (slots < leaves), row_counts[...].astype(F32), leaves * B)
    null_rows(table, leaves * B)

    def step(i, carry):
        for copy in copies(pairs, sems, i, GROUP):
            copy.wait()
        for q in range(GROUP):
            c = i * GROUP + q
            where = pl.ds(pl.multiple_of(c * B, B), B)
            source, target = features(points[:, where])
            wanted[c] = target
            x = masked(rhs[:, where], counts[c])
            table[where, :] = jnp.concatenate([source, *split(x)], axis=0).T
        return carry

    lax.fori_loop(0, steps, step, 0)


def near_scratch():
    return [pltpu.VMEM((B, 2 * K), BF16)] * UNROLL + [pltpu.VMEM((B, B), BF16)] * (2 * UNROLL)


def list_shapes(leaves):
    width = -(-(leaves * NEAR + UNROLL) // 128) * 128
    return [jax.ShapeDtypeStruct((8, width), jnp.int32), jax.ShapeDtypeStruct((leaves, SPAN), jnp.int32)]


def to_scalars(vector, scalar, sems):
    made = [pltpu.make_async_copy(vector[q], scalar[q], sems.at[q]) for q in range(2)]
    for copy in made:
        copy.start()
    for copy in made:
        copy.wait()


def near_own(leaves, boxes, far_points, far_rhs, near, row_counts, scalars, wanted, out, tick, table, points, rhs, items_v, rows_v, items, rows_of, sems, list_sems, *scratch):
    kept, highs, lows = scratch[:UNROLL], scratch[UNROLL : 2 * UNROLL], scratch[2 * UNROLL :]
    counts, _, _, offset, _, _ = parts(scalars, leaves, boxes)
    own_table(leaves, far_points, far_rhs, near, row_counts, counts, offset, wanted, items_v, rows_v, tick, table, points, rhs, sems)
    to_scalars((items_v, rows_v), (items, rows_of), list_sems)
    out[...] = jnp.zeros_like(out)
    near_items(items, rows_of, table, wanted, out, kept, highs, lows)


def halo_table(leaves, left, right, near, *refs):
    *sent, offset, table, items, rows_of = refs
    odd = offset[3] & 1
    across = offset[3] ^ (offset[3] - 1 + 2 * odd)
    row = [x[q, K + 3 : K + 4, :leaves] for x, q in [(sent[0], 1)] + [(x, 1) for x in sent[1:]]]
    far_row = row[-1]
    for at in range(1, len(row) - 1):
        far_row = jnp.where(across == 2 * at + 1, row[at], far_row)
    tails = jnp.where(odd == 1, row[0], far_row)[:, leaves - REACH :]
    heads = jnp.where(odd == 1, far_row, row[0])[:, :REACH]
    counts = jnp.concatenate([tails, heads], axis=1)
    lane = lax.broadcasted_iota(jnp.int32, counts.shape, 1)
    slot = lax.broadcasted_iota(jnp.int32, (R, B), 1).astype(F32)
    null_rows(table, 2 * REACH * B)
    for part, data in ((0, left), (1, right)):

        def step(i, carry, part=part, data=data):
            for q in range(8):
                c = i * 8 + q
                where = pl.ds(pl.multiple_of(c * B, B), B)
                count = jnp.sum(jnp.where(lane == part * REACH + c, counts, 0.0), axis=1, keepdims=True)
                x = jnp.where(slot < count, data[:R, where], 0.0)
                source, _ = features(data[R : R + 3, where], False)
                to = pl.ds(pl.multiple_of((part * REACH + c) * B, B), B)
                table[to, :] = jnp.concatenate([source, *split(x)], axis=0).T
            return carry

        lax.fori_loop(0, REACH // 8, step, 0)
    relative = near[...] - offset[2]
    before = relative < 0
    taken = before | (relative >= leaves)
    slots = jnp.where(before, relative + REACH, relative - leaves + REACH)
    items[...], rows_of[...] = lists(slots, taken, counts, 2 * REACH * B)


def near_halo(leaves, boxes, n_sent, left, right, near, *refs):
    sent, (scalars, wanted, out, table, items_v, rows_v, items, rows_of, list_sems, *scratch) = refs[:n_sent], refs[n_sent:]
    kept, highs, lows = scratch[:UNROLL], scratch[UNROLL : 2 * UNROLL], scratch[2 * UNROLL :]
    offset = parts(scalars, leaves, boxes)[3]
    halo_table(leaves, left, right, near, *sent, offset, table, items_v, rows_v)
    to_scalars((items_v, rows_v), (items, rows_of), list_sems)
    out[...] = jnp.zeros_like(out)
    near_items(items, rows_of, table, wanted, out, kept, highs, lows)


def couple(t_nodes, s_nodes, expansions):
    tiles = []
    for s in s_nodes:
        d = [t_nodes[q] - s[q : q + 1] for q in range(3)]
        tiles.append(lax.rsqrt(1.0 + (d[0] * d[0] + d[1] * d[1] + d[2] * d[2])))
    high, low = split(jnp.concatenate(tiles, axis=1))
    r = dot(jnp.concatenate([high, low], axis=0), expansions)
    return r[:K, :R] + r[:K, R:] + r[K:, :R]


def columns(nodes):
    padded = jnp.concatenate([nodes * 4.0, jnp.zeros((5, nodes.shape[1]), F32)], axis=0)
    return padded.T


def downward(leaves, boxes, coarse, n_dev, n_grp, scalars, *refs):
    counts, parents, uppers, where_am, far_one, far_two = parts(scalars, leaves, boxes)
    sent, refs = refs[: n_dev // 2], refs[n_dev // 2 :]
    tops, refs = refs[: n_grp // 2], refs[n_grp // 2 :]
    basis, transfer, lower, nodes_one, nodes_two, near, more, far_out = refs[:8]
    m_one, m_two, n_one, n_two, c_one, c_two, l_two, g_left, g_right, out, leaf_g, sems = refs[8:]
    box_base, coarse_base, _, dev, grp, group_base = [where_am[q] for q in range(6)]

    for k in range(n_dev):
        at = lax.bitwise_xor(dev, k)
        data = sent[k // 2][k % 2]
        for b in range(boxes):
            m_one[at * boxes + b] = jnp.concatenate(split(data[:K, b * R : (b + 1) * R]), axis=1)
            n_one[at * boxes + b] = data[K : K + 8, b * K : (b + 1) * K] * 4.0
    for k in range(n_grp):
        at = lax.bitwise_xor(grp, k)
        data = tops[k // 2][k % 2]
        for b in range(coarse):
            m_two[at * coarse + b] = jnp.concatenate(split(data[:, b * R : (b + 1) * R]), axis=1)
    for b in range(n_grp * coarse):
        n_two[b, :3] = nodes_two[:, b * K : (b + 1) * K] * 4.0
    c_one[...] = columns(nodes_one[...])
    c_two[...] = columns(nodes_two[...])

    def tiles(nodes, index):
        return [
            jnp.concatenate([nodes[index[q]], nodes[index[q + 1]]], axis=1) for q in range(0, len(index), 2)
        ]

    for t in range(coarse):
        a = coarse_base + t
        index = [far_two[a, q] for q in range(FAR2)]
        start = pl.ds(pl.multiple_of(a * K, K), K)
        t_nodes = [c_two[start, q : q + 1] for q in range(3)]
        l_two[t] = couple(t_nodes, tiles(n_two, index), jnp.concatenate([m_two[q] for q in index], axis=0))

    zero = jnp.zeros((K, R), BF16)
    for t in range(boxes):
        index = [far_one[t, q] - group_base for q in range(FAR1)]
        t_nodes = [c_one[t * K : (t + 1) * K, q : q + 1] for q in range(3)]
        g = couple(t_nodes, tiles(n_one, index), jnp.concatenate([m_one[q] for q in index], axis=0))
        chosen = jnp.concatenate(split(l_two[uppers[t] - coarse_base]), axis=1)
        f_two = jnp.concatenate(split(lower[:, t * K : (t + 1) * K]), axis=0)
        r = dot(f_two, chosen)
        g = g + (r[:K, :R] + r[:K, R:] + r[K:, :R])
        high, low = split(g)
        g_left[t] = jnp.concatenate([high, zero, low, zero], axis=1)
        g_right[t] = jnp.concatenate([zero, high, zero, low], axis=1)

    def lower_pair(at):
        e_two = jnp.concatenate(split(transfer[:, pl.ds(pl.multiple_of(at * 2 * K, 2 * K), 2 * K)]), axis=0)
        p_zero = parents[at * 2] - box_base
        p_one = parents[at * 2 + 1] - box_base
        r = dot(e_two, jnp.concatenate([g_left[p_zero], g_right[p_one]], axis=0))
        leaf_g[at] = r[:K, : 2 * R] + r[:K, 2 * R :] + r[K:, : 2 * R]

    def pair(at):
        g = leaf_g[at]
        turned = jnp.concatenate([g, g], axis=0).T
        high, low = split(turned)
        for side in range(2):
            c = at * 2 + side
            where = pl.ds(pl.multiple_of(c * B, B), B)
            b_two = jnp.concatenate(split(basis[:, where]), axis=0)
            rows = slice(side * R, (side + 1) * R)
            f = dot(jnp.concatenate([high[rows], low[rows]], axis=0), b_two)
            out[:, where] = masked((near[c] + more[c]) + (f[:R] + f[R:]), counts[c])

    def lower_step(i, carry):
        for q in range(GROUP // 2):
            lower_pair(i * (GROUP // 2) + q)
        return carry

    lax.fori_loop(0, near.shape[0] // GROUP, lower_step, 0)
    pairs = ((out, far_out, B),)
    steps = near.shape[0] // GROUP

    def step(i, carry):
        for q in range(GROUP // 2):
            pair(i * (GROUP // 2) + q)
        copies(pairs, sems, i, GROUP)[0].start()
        return carry

    lax.fori_loop(0, steps, step, 0)
    for i in range(steps):
        copies(pairs, sems, i, GROUP)[0].wait()


def swapped(x, axis, by):
    return lax.ppermute(x, axis, [(i, i ^ by) for i in range(lax.axis_size(axis))])


def local(
    points,
    rhs,
    leaf_count,
    near_list,
    leaf_basis,
    leaf_transfer,
    leaf_parent,
    nodes1,
    box_transfer,
    box_parent,
    far1,
    nodes2,
    far2,
):
    leaves = leaf_count.shape[0]
    n_dev = lax.axis_size("dev")
    n_grp = lax.axis_size("grp")
    grp = lax.axis_index("grp")
    dev = lax.axis_index("dev")
    device = grp * n_dev + dev
    boxes = nodes1.shape[1] // K
    coarse = boxes * n_dev // CHILD
    width = REACH * B
    shape = jax.ShapeDtypeStruct

    up = [(i, i + 1) for i in range(n_dev - 1)]
    down = [(i + 1, i) for i in range(n_dev - 1)]

    hbm = pl.BlockSpec(memory_space=pltpu.HBM)
    head, tail = pl.pallas_call(
        pack,
        in_specs=[hbm, vmem()],
        out_specs=[vmem()] * 2,
        out_shape=[shape((R + 3, width), F32)] * 2,
        scratch_shapes=[pltpu.SemaphoreType.DMA((2,))],
        compiler_params=params(),
        name="pack",
    )(rhs, points)
    before = lax.ppermute(tail, "dev", up)
    after = lax.ppermute(head, "dev", down)

    where_am = jnp.stack([device * boxes, grp * coarse, device * leaves, dev, grp, grp * boxes * n_dev]).astype(
        jnp.int32
    )
    scalars = jnp.concatenate(
        [leaf_count, leaf_parent, box_parent, where_am, far1.reshape(-1), far2.reshape(-1)]
    )
    listed = list_shapes(leaves)
    list_scratch = [
        *[pltpu.VMEM(x.shape, x.dtype) for x in listed],
        *[pltpu.SMEM(x.shape, x.dtype) for x in listed],
    ]
    sent = pl.pallas_call(
        lambda *refs: upward(boxes, coarse, leaves, *refs),
        in_specs=[hbm] * 3 + [vmem()] * 3 + [smem()],
        out_specs=vmem(),
        out_shape=shape((K + 8, (boxes + coarse) * R), F32),
        scratch_shapes=[
            pltpu.VMEM((boxes, R, 2 * K), F32),
            pltpu.VMEM((boxes, R, 2 * K), F32),
            pltpu.VMEM((coarse, R, K), F32),
            pltpu.VMEM(rhs.shape, F32),
            pltpu.VMEM(leaf_basis.shape, F32),
            pltpu.VMEM(leaf_transfer.shape, F32),
            pltpu.VMEM((leaves, R, K), F32),
            pltpu.SemaphoreType.DMA((leaves // GROUP, 3)),
        ],
        compiler_params=params(LARGE),
        cost_estimate=cost(40),
        name="upward",
    )(
        rhs,
        leaf_basis,
        leaf_transfer,
        nodes1,
        box_transfer,
        leaf_count.reshape(1, leaves),
        scalars,
    )

    two = jnp.stack([sent, swapped(sent, "dev", 1)])
    all_sent = [two] + [swapped(two, "dev", k) for k in range(2, n_dev, 2)]

    wanted, near, tick = pl.pallas_call(
        lambda *refs: near_own(leaves, boxes, *refs),
        in_specs=[hbm] * 2 + [vmem()] * 2 + [smem()],
        out_specs=[vmem()] * 3,
        out_shape=[shape((leaves, K, B), BF16), shape((leaves, R, B), F32), shape((8, 128), F32)],
        scratch_shapes=[
            pltpu.VMEM((leaves * B + ROWS, 2 * K), BF16),
            pltpu.VMEM(points.shape, F32),
            pltpu.VMEM(rhs.shape, F32),
            *list_scratch,
            pltpu.SemaphoreType.DMA((leaves // GROUP, 2)),
            pltpu.SemaphoreType.DMA((2,)),
            *near_scratch(),
        ],
        compiler_params=params(LARGE),
        cost_estimate=cost(1),
        name="near_own",
    )(points, rhs, near_list, leaf_count.reshape(1, leaves), scalars)

    part = sum(x[q, :K, boxes * R :] for x in all_sent for q in range(2))
    part = part + tick[0, 0]
    part_other = swapped(part, "grp", 1)

    tops_two = jnp.stack([part, part_other])
    tops = [tops_two] + [swapped(tops_two, "grp", k) for k in range(2, n_grp, 2)]

    more = pl.pallas_call(
        lambda *refs: near_halo(leaves, boxes, n_dev // 2, *refs),
        in_specs=[vmem()] * (3 + n_dev // 2) + [smem()] + [vmem()],
        out_specs=vmem(),
        out_shape=shape((leaves, R, B), F32),
        scratch_shapes=[
            pltpu.VMEM((2 * REACH * B + ROWS, 2 * K), BF16),
            *list_scratch,
            pltpu.SemaphoreType.DMA((2,)),
            *near_scratch(),
        ],
        compiler_params=params(LARGE),
        cost_estimate=cost(1),
        name="near_halo",
    )(before, after, near_list, *all_sent, scalars, wanted)

    total_coarse = nodes2.shape[1] // K
    return pl.pallas_call(
        lambda *refs: downward(leaves, boxes, coarse, n_dev, n_grp, *refs),
        in_specs=[smem()] + [vmem()] * (n_dev // 2 + n_grp // 2 + 7),
        out_specs=hbm,
        out_shape=shape((R, leaves * B), F32),
        scratch_shapes=[
            pltpu.VMEM((boxes * n_dev, K, 2 * R), BF16),
            pltpu.VMEM((total_coarse, K, 2 * R), BF16),
            pltpu.VMEM((boxes * n_dev, 8, K), F32),
            pltpu.VMEM((total_coarse, 8, K), F32),
            pltpu.VMEM((boxes * K, 8), F32),
            pltpu.VMEM((total_coarse * K, 8), F32),
            pltpu.VMEM((coarse, K, R), F32),
            pltpu.VMEM((boxes, K, 4 * R), BF16),
            pltpu.VMEM((boxes, K, 4 * R), BF16),
            pltpu.VMEM((R, leaves * B), F32),
            pltpu.VMEM((leaves // 2, K, 2 * R), F32),
            pltpu.SemaphoreType.DMA((leaves // GROUP, 1)),
        ],
        compiler_params=params(LARGE),
        cost_estimate=cost(15),
        name="downward",
    )(
        scalars,
        *all_sent,
        *tops,
        leaf_basis,
        leaf_transfer,
        box_transfer,
        nodes1,
        nodes2,
        near,
        more,
    )


def solution(mesh):
    placed = (
        P(None, ("grp", "dev")),
        P(None, ("grp", "dev")),
        P(("grp", "dev")),
        P(("grp", "dev"), None),
        P(None, ("grp", "dev")),
        P(None, ("grp", "dev")),
        P(("grp", "dev")),
        P(None, ("grp", "dev")),
        P(None, ("grp", "dev")),
        P(("grp", "dev")),
        P(("grp", "dev"), None),
        P(),
        P(),
    )
    return jax.shard_map(
        local, mesh=mesh, in_specs=placed, out_specs=P(None, ("grp", "dev")), check_vma=False
    )
```
